256 devices in a mesh: frame: 8 (over x, y_lo), patch: 32 (over y_hi, z, core).
Axes of the slice: x: 4, y: 4 (y_hi: 2, y_lo: 2; y = y_hi * 2 + y_lo), z: 8, core: 2. Of those that a mesh axis runs over, the one named last changes fastest.
Arguments:
- queries: bfloat16 [8, 4096, 1024], P('frame', 'patch'), may hold values from -8 to 8
- key_states: bfloat16 [8, 4096, 1024], P('frame', 'patch'), may hold values from -8 to 8
- value_states: bfloat16 [8, 4096, 1024], P('frame', 'patch'), may hold values from -6 to 6
- out_grad: bfloat16 [8, 4096, 1024], P('frame', 'patch'), may hold values from -6 to 6
Outputs:
- grad_queries: bfloat16 [8, 4096, 1024], P('frame', 'patch')
- grad_keys: bfloat16 [8, 4096, 1024], P('frame', 'patch')
- grad_values: bfloat16 [8, 4096, 1024], P('frame', 'patch')
The draws below stay inside these ranges and needn't reach their ends.
All inputs are finite; a program needn't handle non-finite values.
Results may differ from the reference program's by a relative error of at most 0.0076.
Values may be sent and summed in bfloat16 or wider, within the bound.
No kernel may reach another device: no remote copies, remote signals or barrier semaphores. Data moves between devices by JAX's collectives and lax.ppermute only.
A program may use at most 64 MiB of HBM per device.

```python
import math
import jax
import jax.numpy as jnp
from jax import lax

HEADS = 8
HD = 128
FR_DEV = 1
PA_DEV = 128
FRAMES = 8
PATCHES = 4096
N_FRAME = 8
N_PATCH = 32


def draw_queries(key, part):
    return drawn_draw_with(key, 1)


def draw_key_states(key, part):
    return drawn_draw_with(key, 2)


def drawn_draw_with(key, salt):
    own_key = jax.random.fold_in(key, salt)
    key_base = jax.random.fold_in(own_key, 0)
    result = jnp.clip(jax.random.normal(key_base, (FRAMES, PATCHES, HEADS * HD), jnp.float32), -6.0, 6.0)
    return result.astype(jnp.bfloat16)


def level_of(rng, shape, shards, low, high):
    factor_of = 1.0
    for position, shards_of in shards:
        steps = jax.random.uniform(jax.random.fold_in(jax.random.fold_in(rng, 6), position), (shards_of,), jnp.float32, low / len(shards), high / len(shards))
        factor_of = factor_of * jnp.repeat(jnp.exp(steps), shape[position] // shards_of).reshape((-1,) + (1,) * (len(shape) - 1 - position))
    return factor_of


def noise(key, extent, deviation, limit, shards=(), kind=jnp.bfloat16):
    array = deviation * jax.random.normal(key, extent, jnp.float32)
    if shards:
        array = array * level_of(key, extent, shards, -0.22, 0.18)
    return jnp.clip(array, -limit, limit).astype(kind)


def setup_inputs(seed: int = 0) -> dict:
    key_list = jax.random.split(jax.random.key(seed), 5)
    queries = draw_queries(jax.random.fold_in(key_list[4], 71), 0)
    key_states = draw_key_states(jax.random.fold_in(key_list[4], 71), 0)
    value_states = noise(key_list[2], (FRAMES, PATCHES, HEADS * HD), 1.0, 6.0, ((0, 8), (1, 32)))
    out_grad = noise(key_list[3], (FRAMES, PATCHES, HEADS * HD), 1.0, 6.0, ((0, 8), (1, 32)))
    return {"queries": queries, "key_states": key_states, "value_states": value_states, "out_grad": out_grad}


def to_blocks(tensor):
    channels = tensor.shape[-1]
    shaped = tensor.reshape(N_FRAME, FR_DEV, N_PATCH, PA_DEV, channels).transpose(0, 2, 1, 3, 4)
    return shaped.reshape(N_FRAME, N_PATCH, FR_DEV * PA_DEV, channels)

def from_blocks(blocked):
    channels = blocked.shape[-1]
    shaped = blocked.reshape(N_FRAME, N_PATCH, FR_DEV, PA_DEV, channels).transpose(0, 2, 1, 3, 4)
    return shaped.reshape(FRAMES, PATCHES, channels)

def window_of(blocked, frame_pos, patch_pos, axis_pos):
    pieces = []
    for frame_step in (-1, 0, 1):
        for patch_step in (-1, 0, 1):
            pieces.append(blocked[(frame_pos + frame_step) % N_FRAME, (patch_pos + patch_step) % N_PATCH])
    return jnp.concatenate(pieces, axis=axis_pos)

def heads_of(tensor):
    return tensor.reshape(tensor.shape[0], HEADS, HD).astype(jnp.float32)

def reference(queries, key_states, value_states, out_grad):
    scale_factor = 1.0 / math.sqrt(HD)
    query_blocks = to_blocks(queries)
    key_blocks = to_blocks(key_states)
    value_blocks = to_blocks(value_states)
    grad_blocks = to_blocks(out_grad)
    block_total = N_FRAME * N_PATCH
    tok_rows = FR_DEV * PA_DEV

    def statistics(block_index):
        frame_pos = block_index // N_PATCH
        patch_pos = block_index % N_PATCH
        query_here = heads_of(query_blocks[frame_pos, patch_pos])
        grad_here = heads_of(grad_blocks[frame_pos, patch_pos])
        key_win = heads_of(window_of(key_blocks, frame_pos, patch_pos, 0))
        value_win = heads_of(window_of(value_blocks, frame_pos, patch_pos, 0))
        scores = jnp.einsum('thd,shd->hts', query_here, key_win) * scale_factor
        log_total = jax.nn.logsumexp(scores, axis=-1)
        prob_half = jnp.exp(scores - log_total[:, :, None]).astype(jnp.bfloat16)
        forward_out = jnp.einsum('hts,shd->thd', prob_half.astype(jnp.float32), value_win)
        row_delta = lax.optimization_barrier(jnp.sum(grad_here * forward_out, axis=-1)).T
        return (log_total, row_delta)
    indices = jnp.arange(block_total, dtype=jnp.int32)
    total_all, delta_all = lax.map(statistics, indices)
    total_all = total_all.reshape(N_FRAME, N_PATCH, HEADS, tok_rows)
    delta_all = delta_all.reshape(N_FRAME, N_PATCH, HEADS, tok_rows)

    def query_side(block_index):
        frame_pos = block_index // N_PATCH
        patch_pos = block_index % N_PATCH
        query_here = heads_of(query_blocks[frame_pos, patch_pos])
        grad_here = heads_of(grad_blocks[frame_pos, patch_pos])
        key_win = heads_of(window_of(key_blocks, frame_pos, patch_pos, 0))
        value_win = heads_of(window_of(value_blocks, frame_pos, patch_pos, 0))
        scores = jnp.einsum('thd,shd->hts', query_here, key_win) * scale_factor
        prob_full = jnp.exp(scores - total_all[frame_pos, patch_pos][:, :, None])
        grad_prob = jnp.einsum('thd,shd->hts', grad_here, value_win)
        dscore = (prob_full * (grad_prob - delta_all[frame_pos, patch_pos][:, :, None])).astype(jnp.bfloat16)
        grad_query = jnp.einsum('hts,shd->thd', dscore.astype(jnp.float32), key_win) * scale_factor
        return grad_query.astype(jnp.bfloat16).reshape(tok_rows, HEADS * HD)

    def key_side(block_index):
        frame_pos = block_index // N_PATCH
        patch_pos = block_index % N_PATCH
        key_here = heads_of(key_blocks[frame_pos, patch_pos])
        value_here = heads_of(value_blocks[frame_pos, patch_pos])
        query_win = heads_of(window_of(query_blocks, frame_pos, patch_pos, 0))
        grad_win = heads_of(window_of(grad_blocks, frame_pos, patch_pos, 0))
        total_win = window_of(total_all, frame_pos, patch_pos, 1)
        delta_win = window_of(delta_all, frame_pos, patch_pos, 1)
        scores = jnp.einsum('thd,shd->hts', query_win, key_here) * scale_factor
        prob_full = jnp.exp(scores - total_win[:, :, None])
        prob_half = prob_full.astype(jnp.bfloat16)
        grad_prob = jnp.einsum('thd,shd->hts', grad_win, value_here)
        dscore = (prob_full * (grad_prob - delta_win[:, :, None])).astype(jnp.bfloat16)
        grad_value = jnp.einsum('hts,thd->shd', prob_half.astype(jnp.float32), grad_win)
        grad_key = jnp.einsum('hts,thd->shd', dscore.astype(jnp.float32), query_win) * scale_factor
        return (grad_key.astype(jnp.bfloat16).reshape(tok_rows, HEADS * HD), grad_value.astype(jnp.bfloat16).reshape(tok_rows, HEADS * HD))
    query_grads = lax.map(query_side, indices)
    key_grads, value_grads = lax.map(key_side, indices)
    shape_blocks = (N_FRAME, N_PATCH, tok_rows, HEADS * HD)
    return (from_blocks(query_grads.reshape(shape_blocks)), from_blocks(key_grads.reshape(shape_blocks)), from_blocks(value_grads.reshape(shape_blocks)))
```

```python
import math

import jax
import jax.numpy as jnp
import numpy as np
from jax import lax
from jax.experimental import pallas as pl
from jax.experimental.pallas import tpu as pltpu
from jax.sharding import PartitionSpec as P

HD = 128
BLK = 128
WIDE = 2 * HD
AXES = ("x", "l", "h", "z", "c")
SIZES = (4, 2, 2, 8, 2)
SCALE = 1.0 / math.sqrt(HD)
EXP_SCALE = SCALE * math.log2(math.e)
BF = jnp.bfloat16
F32 = jnp.float32


def make_perm(target):
    pairs = []
    for index in range(math.prod(SIZES)):
        place = [int(v) for v in np.unravel_index(index, SIZES)]
        pairs.append((index, int(np.ravel_multi_index(target(*place), SIZES))))
    return pairs


def ring_z(x, l, h, z, c, step):
    near = z + step
    if 0 <= near < 8:
        return (x, l, h, near, c)
    return (x, 1 - l, 1 - h, near % 8, c)


def up(bit):
    return 2 * bit - 1


CORE = make_perm(lambda x, l, h, z, c: (x, l, h, z, 1 - c))
PAIR = make_perm(lambda x, l, h, z, c: (x, 1 - l, h, z, c))
X_OWN = make_perm(lambda x, l, h, z, c: ((x + up(l)) % 4, l, h, z, c))
X_FAR = make_perm(lambda x, l, h, z, c: ((x - up(l)) % 4, l, h, z, c))
Z_OWN = make_perm(lambda x, l, h, z, c: ring_z(x, l, h, z, c, up(c)))
Z_FAR = make_perm(lambda x, l, h, z, c: ring_z(x, l, h, z, c, -up(c)))


def move(value, perm):
    return lax.ppermute(value, AXES, perm)


KEYS = [(r, s) for r in range(4) for s in range(4)]


def query_runs(r, s):
    rows = [i for i in (1, 2) if abs(i - r) <= 1]
    cols = [j for j in (1, 2) if abs(j - s) <= 1]
    if len(cols) == 2:
        first = (rows[0] - 1) * 2
        return [(first, 2 * len(rows))]
    return [((i - 1) * 2 + cols[0] - 1, 1) for i in rows]


def dot_nt(a, b):
    return lax.dot_general(a, b, (((1,), (1,)), ((), ())), preferred_element_type=F32)


def dot_nn(a, b):
    return lax.dot_general(a, b, (((1,), (0,)), ((), ())), preferred_element_type=F32)


def fold(tile):
    return tile.reshape(BLK // 8, 8, BLK)


def attention_kernel(
    flip, qg1, qg2, kv1, kv2, kv3, kv0, za12, zb12, za30, zb30,
    dq1, dq2, p1, p2, p3, p0, pa12, pb12, pa30, pb30,
    qh, gh, kt, s_s, d_s, p_s, ds_s,
):
    fa = flip[0]
    fb = flip[1]

    def place(r, s, tile_refs, a12, b12, a30, b30):
        if s in (1, 2):
            return tile_refs[r], s - 1
        near, bit = (a12, fa) if s == 3 else (b12, fb)
        far = a30 if s == 3 else b30
        if r in (1, 2):
            return near, bit if r == 1 else 1 - bit
        return far, bit if r == 3 else 1 - bit

    def key_place(r, s):
        return place(r, s, (kv0, kv1, kv2, kv3), za12, zb12, za30, zb30)

    def grad_place(r, s):
        return place(r, s, (p0, p1, p2, p3), pa12, pb12, pa30, pb30)

    for head in range(2):
        lanes = slice(head * HD, (head + 1) * HD)
        for i, (ref, j) in enumerate(((qg1, 0), (qg1, 1), (qg2, 0), (qg2, 1))):
            rows = slice(i * BLK, (i + 1) * BLK)
            qh[rows, :] = ref[j, 0, :, lanes]
            gh[rows, :] = ref[j, 1, :, lanes]
        peak = [None] * 4
        for u, (r, s) in enumerate(KEYS):
            ref, index = key_place(r, s)
            key = ref[index, 0, :, lanes]
            value = ref[index, 1, :, lanes]
            kt[:, u * BLK : (u + 1) * BLK] = key.T
            urows = slice(u * BLK, (u + 1) * BLK)
            for first, count in query_runs(r, s):
                part = slice(first * BLK, (first + count) * BLK)
                scores = dot_nt(key, qh[part, :])
                s_s[urows, part] = scores
                d_s[urows, part] = dot_nt(value, gh[part, :])
                for k in range(count):
                    top = jnp.max(fold(scores[:, k * BLK : (k + 1) * BLK]), axis=0)
                    q = first + k
                    peak[q] = top if peak[q] is None else jnp.maximum(peak[q], top)
        for q in range(4):
            qr, qs = q // 2 + 1, q % 2 + 1
            part = slice(q * BLK, (q + 1) * BLK)
            window = [r * 4 + s for r in range(qr - 1, qr + 2) for s in range(qs - 1, qs + 2)]
            top = jnp.max(peak[q], axis=0, keepdims=True) * EXP_SCALE
            total8 = jnp.zeros((8, BLK), F32)
            delta8 = jnp.zeros((8, BLK), F32)
            for u in window:
                urows = slice(u * BLK, (u + 1) * BLK)
                e = jnp.exp2(s_s[urows, part] * EXP_SCALE - top)
                s_s[urows, part] = e
                total8 = total8 + jnp.sum(fold(e), axis=0)
                delta8 = delta8 + jnp.sum(fold(e * d_s[urows, part]), axis=0)
            inverse = 1.0 / jnp.sum(total8, axis=0, keepdims=True)
            delta = jnp.sum(delta8, axis=0, keepdims=True) * inverse
            for u in window:
                urows = slice(u * BLK, (u + 1) * BLK)
                prob = s_s[urows, part] * inverse
                p_s[urows, part] = prob.astype(BF)
                ds_s[urows, part] = (prob * (d_s[urows, part] - delta)).astype(BF)
        for u, (r, s) in enumerate(KEYS):
            urows = slice(u * BLK, (u + 1) * BLK)
            dkey = None
            for first, count in query_runs(r, s):
                part = slice(first * BLK, (first + count) * BLK)
                one = dot_nn(ds_s[urows, part], qh[part, :])
                two = dot_nn(p_s[urows, part], gh[part, :])
                dkey, dvalue = (one, two) if dkey is None else (dkey + one, dvalue + two)
            ref, index = grad_place(r, s)
            ref[index, 0, :, lanes] = (dkey * SCALE).astype(ref.dtype)
            ref[index, 1, :, lanes] = dvalue.astype(ref.dtype)
        for q in range(4):
            qr, qs = q // 2 + 1, q % 2 + 1
            part = slice(q * BLK, (q + 1) * BLK)
            acc = None
            for r in range(qr - 1, qr + 2):
                u = r * 4 + qs - 1
                long = slice(u * BLK, (u + 3) * BLK)
                one = dot_nn(kt[:, long], ds_s[long, part])
                acc = one if acc is None else acc + one
            out = dq1 if qr == 1 else dq2
            out[qs - 1, :, lanes] = (acc * SCALE).T.astype(BF)


def attention(flip, *arrays):
    vmem = pl.BlockSpec(memory_space=pltpu.VMEM)
    smem = pl.BlockSpec(memory_space=pltpu.SMEM)
    dq = jax.ShapeDtypeStruct((2, BLK, WIDE), BF)
    wide = jax.ShapeDtypeStruct((2, 2, BLK, WIDE), F32)
    half = jax.ShapeDtypeStruct((2, 2, BLK, WIDE), BF)
    return pl.pallas_call(
        attention_kernel,
        out_shape=[dq] * 2 + [wide] * 4 + [half] * 4,
        in_specs=[smem] + [vmem] * 10,
        out_specs=[vmem] * 10,
        scratch_shapes=[
            pltpu.VMEM((4 * BLK, HD), BF),
            pltpu.VMEM((4 * BLK, HD), BF),
            pltpu.VMEM((HD, 16 * BLK), BF),
            pltpu.VMEM((16 * BLK, 4 * BLK), F32),
            pltpu.VMEM((16 * BLK, 4 * BLK), F32),
            pltpu.VMEM((16 * BLK, 4 * BLK), BF),
            pltpu.VMEM((16 * BLK, 4 * BLK), BF),
        ],
        compiler_params=pltpu.CompilerParams(vmem_limit_bytes=48 * 1024 * 1024),
        cost_estimate=pl.CostEstimate(
            flops=1_500_000_000, bytes_accessed=8 * 1024 * 1024, transcendentals=1_200_000
        ),
    )(flip, *arrays)


def on_device(queries, key_states, value_states, out_grad):
    l = lax.axis_index("l")
    h = lax.axis_index("h")
    z = lax.axis_index("z")
    c = lax.axis_index("c")
    group = l ^ h
    low_end = z == 0
    high_end = z == 7
    flip = jnp.stack(
        [
            jnp.where(c == 1, low_end, high_end).astype(jnp.int32),
            jnp.where(c == 1, high_end, low_end).astype(jnp.int32),
        ]
    )

    def lanes(array, start, width):
        return lax.dynamic_slice_in_dim(array, start, width, axis=array.ndim - 1)

    def to_tile(first, second):
        both = (first[0], second[0])
        away = jnp.stack([lanes(a, (1 - c) * 512, 512) for a in both])
        came = move(away, CORE)
        other = jnp.stack(
            [
                jnp.stack([lanes(a, c * 512 + (1 - group) * WIDE, WIDE) for a in both]),
                lanes(came, (1 - group) * WIDE, WIDE),
            ]
        )
        mine = jnp.stack(
            [
                jnp.stack([lanes(a, c * 512 + group * WIDE, WIDE) for a in both]),
                lanes(came, group * WIDE, WIDE),
            ]
        )
        return mine, other

    kv1, kv_other = to_tile(key_states, value_states)
    kv2 = move(kv_other, PAIR)
    kv3 = move(kv1, X_OWN)
    qg1, qg_other = to_tile(queries, out_grad)
    qg2 = move(qg_other, PAIR)
    kv0 = move(kv2, X_FAR)
    za12 = move(jnp.stack([kv1[0], kv2[0]]), Z_OWN)
    zb12 = move(jnp.stack([kv1[1], kv2[1]]), Z_FAR)
    za30 = move(jnp.stack([kv3[0], kv0[0]]), Z_OWN)
    zb30 = move(jnp.stack([kv3[1], kv0[1]]), Z_FAR)

    dq1, dq2, p1, p2, p3, p0, pa12, pb12, pa30, pb30 = attention(
        flip, qg1, qg2, kv1, kv2, kv3, kv0, za12, zb12, za30, zb30
    )

    ra30 = move(pa30, Z_FAR)
    rb30 = move(pb30, Z_OWN)
    ra12 = move(pa12, Z_FAR)
    rb12 = move(pb12, Z_OWN)
    dq_pair = move(dq2, PAIR)

    def with_sides(part, near, far, row):
        return part + jnp.stack([near[row], far[row]]).astype(F32)

    r0 = move(with_sides(p0, ra30, rb30, 1).astype(BF), X_OWN)
    r3 = move(with_sides(p3, ra30, rb30, 0).astype(BF), X_FAR)
    row2 = (with_sides(p2, ra12, rb12, 1) + r0.astype(F32)).astype(BF)
    row1 = (with_sides(p1, ra12, rb12, 0) + r3.astype(F32)).astype(BF)
    row_pair = move(row2, PAIR)

    own = jnp.concatenate([dq1[:, None], row1], axis=1)
    pair = jnp.concatenate([dq_pair[:, None], row_pair], axis=1)
    quad = jnp.where(
        group == 0,
        jnp.concatenate([own, pair], axis=-1),
        jnp.concatenate([pair, own], axis=-1),
    )
    came = move(quad[1], CORE)
    kept = quad[0]
    full = jnp.where(
        c == 0,
        jnp.concatenate([kept, came], axis=-1),
        jnp.concatenate([came, kept], axis=-1),
    )
    return full[0][None], full[1][None], full[2][None]


def solution(mesh):
    fine = jax.sharding.Mesh(mesh.devices.reshape(SIZES), AXES)
    placed = P(("x", "l"), ("h", "z", "c"), None)
    return jax.shard_map(
        on_device,
        mesh=fine,
        in_specs=(placed,) * 4,
        out_specs=(placed,) * 3,
        check_vma=False,
    )
```

```python
import math

import jax
import jax.numpy as jnp
import numpy as np
from jax import lax
from jax.experimental import pallas as pl
from jax.experimental.pallas import tpu as pltpu
from jax.sharding import PartitionSpec as P

HD = 128
BLK = 128
FRAMES = 8
WIN = 3 * BLK
AXES = ("x", "l", "h", "z", "c")
SIZES = (4, 2, 2, 8, 2)
SCALE = 1.0 / math.sqrt(HD)
EXP_SCALE = SCALE * math.log2(math.e)
BF = jnp.bfloat16
F32 = jnp.float32
VMEM = pl.BlockSpec(memory_space=pltpu.VMEM)
HBM = pl.BlockSpec(memory_space=pltpu.HBM)
SMEM = pl.BlockSpec(memory_space=pltpu.SMEM)
Q, K, V, G = range(4)


def make_perm(target):
    pairs = []
    for index in range(math.prod(SIZES)):
        place = [int(v) for v in np.unravel_index(index, SIZES)]
        pairs.append((index, int(np.ravel_multi_index(target(*place), SIZES))))
    return pairs


def over_z(x, l, h, z, c):
    near = z + 2 * c - 1
    if 0 <= near < 8:
        return (x, l, h, near, 1 - c)
    return (x, 1 - l, 1 - h, near % 8, 1 - c)


CORE = make_perm(lambda x, l, h, z, c: (x, l, h, z, 1 - c))
OVER_Z = make_perm(over_z)


def move(value, perm):
    return lax.ppermute(value, AXES, perm)


def dot_nt(a, b):
    return lax.dot_general(a, b, (((1,), (1,)), ((), ())), preferred_element_type=F32)


def dot_nn(a, b):
    return lax.dot_general(a, b, (((1,), (0,)), ((), ())), preferred_element_type=F32)


def fold(tile):
    return tile.reshape(BLK // 8, 8, BLK)


def near(frame):
    return [(frame + step) % FRAMES for step in (-1, 0, 1)]


def bytes_of(shapes):
    return sum(math.prod(s.shape) * s.dtype.itemsize for s in shapes)


def call(kernel, outs, args, scratch=(), smem=0, flops=0, space=VMEM, limit=32):
    return pl.pallas_call(
        kernel,
        out_shape=outs,
        in_specs=[SMEM] * smem + [space] * (len(args) - smem),
        out_specs=[VMEM] * len(outs),
        scratch_shapes=list(scratch),
        compiler_params=pltpu.CompilerParams(vmem_limit_bytes=limit * 1024 * 1024 if limit else None),
        cost_estimate=pl.CostEstimate(
            flops=flops, bytes_accessed=bytes_of(args) + bytes_of(outs), transcendentals=0
        ),
    )(*args)


def pack_kernel(swap, q, k, v, g, out, held, sems):
    half = BLK // 2
    copies = {}
    for place, ref in enumerate((q, k, v, g)):
        for part in range(2):
            rows = pl.ds(part * half, half)
            copies[place, part] = pltpu.make_async_copy(
                ref.at[0, rows], held.at[place, rows], sems.at[place, part]
            )
            copies[place, part].start()
    for (place, part), copy in copies.items():
        copy.wait()
        rows = slice(part * half, (part + 1) * half)
        for head in range(FRAMES):
            out[head ^ swap[0], place, rows] = held[place, rows, head * HD : (head + 1) * HD]


def unpack_kernel(swap, tile, dq, dk, dv):
    for place, ref in enumerate((dq, dk, dv)):
        for head in range(FRAMES):
            ref[0, :, head * HD : (head + 1) * HD] = tile[head ^ swap[0], place]


def column_sums(tile, f, keys, values, before):
    query = tile[f, Q]
    grad = tile[f, G]
    scores = [dot_nt(key, query) for key in keys]
    top8 = None
    for s in scores:
        one = jnp.max(fold(s), axis=0)
        top8 = one if top8 is None else jnp.maximum(top8, one)
    top = jnp.max(top8, axis=0, keepdims=True) * EXP_SCALE
    if before is not None:
        top = jnp.maximum(top, before[0])
    total8 = jnp.zeros((8, BLK), F32)
    delta8 = jnp.zeros((8, BLK), F32)
    exps = []
    grads = []
    for value, s in zip(values, scores):
        e = jnp.exp2(s * EXP_SCALE - top)
        grad_prob = dot_nt(value, grad)
        total8 = total8 + jnp.sum(fold(e), axis=0)
        delta8 = delta8 + jnp.sum(fold(e * grad_prob), axis=0)
        exps.append(e)
        grads.append(grad_prob)
    total = jnp.sum(total8, axis=0, keepdims=True)
    delta = jnp.sum(delta8, axis=0, keepdims=True)
    if before is not None:
        shrink = jnp.exp2(before[0] - top)
        total = total + before[1] * shrink
        delta = delta + before[2] * shrink
    return (top, total, delta), exps, grads


def near_sums_kernel(tile, core, stats):
    for f in range(FRAMES):
        keys = [tile[u, K] for u in near(f)] + [core[u, 0] for u in near(f)]
        values = [tile[u, V] for u in near(f)] + [core[u, 1] for u in near(f)]
        sums, _, _ = column_sums(tile, f, keys, values, None)
        for i, row in enumerate(sums):
            stats[i, f : f + 1, :] = row


def wrap_queries(tile, qw, gw):
    for i in range(FRAMES + 2):
        rows = slice(i * BLK, (i + 1) * BLK)
        qw[rows, :] = tile[(i - 1) % FRAMES, Q]
        gw[rows, :] = tile[(i - 1) % FRAMES, G]


def far_column_kernel(tile, far, stats, part, ds_by_query, final, qw, gw, p_s, ds_s):
    wrap_queries(tile, qw, gw)
    for f in range(FRAMES):
        keys = [far[u, 0] for u in near(f)]
        values = [far[u, 1] for u in near(f)]
        rows = [stats[i, f : f + 1, :] for i in range(3)]
        (top, total, delta), exps, grads = column_sums(tile, f, keys, values, rows)
        inverse = 1.0 / total
        delta = delta * inverse
        final[0, f : f + 1, :] = top + jnp.log2(total)
        final[1, f : f + 1, :] = delta
        for i, u in enumerate(near(f)):
            lanes = slice((2 - i) * BLK, (3 - i) * BLK)
            prob = exps[i] * inverse
            dscore = (prob * (grads[i] - delta)).astype(BF)
            p_s[u, :, lanes] = prob.astype(BF)
            ds_s[u, :, lanes] = dscore
            ds_by_query[f, i * BLK : (i + 1) * BLK, :] = dscore
    for u in range(FRAMES):
        rows = slice(u * BLK, u * BLK + WIN)
        part[u, 0] = (dot_nn(ds_s[u], qw[rows, :]) * SCALE).astype(BF)
        part[u, 1] = dot_nn(p_s[u], gw[rows, :]).astype(BF)


def near_columns_kernel(
    tile, core, far, ds_far, final, own_part, core_part, dq, qw, gw, kt, p_s, ds_s, dsq
):
    wrap_queries(tile, qw, gw)
    for i in range(FRAMES + 2):
        rows = slice(i * BLK, (i + 1) * BLK)
        u = (i - 1) % FRAMES
        kt[0, :, rows] = tile[u, K].T
        kt[1, :, rows] = core[u, 0].T
        kt[2, :, rows] = far[u, 0].T
    for f in range(FRAMES):
        query = tile[f, Q]
        grad = tile[f, G]
        total = final[0, f : f + 1, :]
        delta = final[1, f : f + 1, :]
        for i, u in enumerate(near(f)):
            lanes = slice((2 - i) * BLK, (3 - i) * BLK)
            for j, (key, value) in enumerate(((tile[u, K], tile[u, V]), (core[u, 0], core[u, 1]))):
                prob = jnp.exp2(dot_nt(key, query) * EXP_SCALE - total)
                dscore = (prob * (dot_nt(value, grad) - delta)).astype(BF)
                p_s[j, u, :, lanes] = prob.astype(BF)
                ds_s[j, u, :, lanes] = dscore
                dsq[j, f, i * BLK : (i + 1) * BLK, :] = dscore
    for u in range(FRAMES):
        rows = slice(u * BLK, u * BLK + WIN)
        for j, out in enumerate((own_part, core_part)):
            out[u, 0] = (dot_nn(ds_s[j, u], qw[rows, :]) * SCALE).astype(out.dtype)
            out[u, 1] = dot_nn(p_s[j, u], gw[rows, :]).astype(out.dtype)
    for f in range(FRAMES):
        rows = slice(f * BLK, f * BLK + WIN)
        acc = dot_nn(kt[0, :, rows], dsq[0, f]) + dot_nn(kt[1, :, rows], dsq[1, f])
        acc = acc + dot_nn(kt[2, :, rows], ds_far[f])
        dq[f] = (acc * SCALE).T.astype(BF)


def add_far_kernel(own_part, far_back, out):
    for u in range(FRAMES):
        for place in range(2):
            out[u, place] = own_part[u, place] + far_back[u, place].astype(F32)


def gather_kernel(part, core_back, dq, out):
    for u in range(FRAMES):
        out[u, 0] = dq[u]
        for place in range(2):
            out[u, 1 + place] = (part[u, place] + core_back[u, place].astype(F32)).astype(BF)


def on_device(queries, key_states, value_states, out_grad):
    swap = lax.axis_index("h").astype(jnp.int32).reshape(1)
    shape = jax.ShapeDtypeStruct
    pair = (FRAMES, 2, BLK, HD)
    window = (FRAMES, BLK, WIN)
    wrapped = pltpu.VMEM(((FRAMES + 2) * BLK, HD), BF)
    mats = 2 * BLK * BLK * HD * FRAMES * 3

    packed = call(
        pack_kernel,
        [shape((FRAMES, 4, BLK, HD), BF)],
        (swap, queries, key_states, value_states, out_grad),
        scratch=(pltpu.VMEM((4, BLK, FRAMES * HD), BF), pltpu.SemaphoreType.DMA((4, 2))),
        smem=1,
        space=HBM,
        limit=0,
    )[0]
    tile = lax.all_to_all(packed, ("x", "l"), 0, 0)
    keys_values = tile[:, K : V + 1]
    far = move(keys_values, OVER_Z)
    core = move(keys_values, CORE)
    stats = call(
        near_sums_kernel, [shape((3, FRAMES, BLK), F32)], (tile, core), flops=4 * mats
    )[0]
    far_part, ds_far, final = call(
        far_column_kernel,
        [
            shape(pair, BF),
            shape((FRAMES, WIN, BLK), BF),
            shape((2, FRAMES, BLK), F32),
        ],
        (tile, far, stats),
        scratch=(wrapped, wrapped, pltpu.VMEM(window, BF), pltpu.VMEM(window, BF)),
        flops=4 * mats,
    )
    far_back = move(far_part, OVER_Z)
    own_part, core_part, dq = call(
        near_columns_kernel,
        [shape(pair, F32), shape(pair, BF), shape((FRAMES, BLK, HD), BF)],
        (tile, core, far, ds_far, final),
        scratch=(
            wrapped,
            wrapped,
            pltpu.VMEM((3, HD, (FRAMES + 2) * BLK), BF),
            pltpu.VMEM((2,) + window, BF),
            pltpu.VMEM((2,) + window, BF),
            pltpu.VMEM((2, FRAMES, WIN, BLK), BF),
        ),
        flops=11 * mats,
    )
    core_back = move(core_part, CORE)
    part = call(add_far_kernel, [shape(pair, F32)], (own_part, far_back), flops=10 * mats)[0]
    grads = call(
        gather_kernel, [shape((FRAMES, 3, BLK, HD), BF)], (part, core_back, dq)
    )[0]
    back = lax.all_to_all(grads, ("x", "l"), 0, 0)
    flat = shape((1, BLK, FRAMES * HD), BF)
    return tuple(call(unpack_kernel, [flat] * 3, (swap, back), smem=1))


def solution(mesh):
    fine = jax.sharding.Mesh(mesh.devices.reshape(SIZES), AXES)
    placed = P(("x", "l"), ("h", "z", "c"), None)
    return jax.shard_map(
        on_device,
        mesh=fine,
        in_specs=(placed,) * 4,
        out_specs=(placed,) * 3,
        check_vma=False,
    )
```

```python
import math

import jax
import jax.numpy as jnp
import numpy as np
from jax import lax
from jax.experimental import pallas as pl
from jax.experimental.pallas import tpu as pltpu
from jax.sharding import PartitionSpec as P

HD = 128
BLK = 128
FRAMES = 8
WIN = 3 * BLK
AXES = ("x", "l", "h", "z", "c")
SIZES = (4, 2, 2, 8, 2)
SCALE = 1.0 / math.sqrt(HD)
EXP_SCALE = SCALE * math.log2(math.e)
BF = jnp.bfloat16
F32 = jnp.float32
VMEM = pl.BlockSpec(memory_space=pltpu.VMEM)
HBM = pl.BlockSpec(memory_space=pltpu.HBM)
SMEM = pl.BlockSpec(memory_space=pltpu.SMEM)


def make_perm(target):
    pairs = []
    for index in range(math.prod(SIZES)):
        place = [int(v) for v in np.unravel_index(index, SIZES)]
        pairs.append((index, int(np.ravel_multi_index(target(*place), SIZES))))
    return pairs


def over_z(x, l, h, z, c):
    near = z + 2 * c - 1
    if 0 <= near < 8:
        return (x, l, h, near, 1 - c)
    return (x, 1 - l, 1 - h, near % 8, 1 - c)


CORE = make_perm(lambda x, l, h, z, c: (x, l, h, z, 1 - c))
OVER_Z = make_perm(over_z)


def move(value, perm):
    return lax.ppermute(value, AXES, perm)


def dot_nt(a, b):
    return lax.dot_general(a, b, (((1,), (1,)), ((), ())), preferred_element_type=F32)


def dot_nn(a, b):
    return lax.dot_general(a, b, (((1,), (0,)), ((), ())), preferred_element_type=F32)


def bytes_of(shapes):
    return sum(math.prod(s.shape) * s.dtype.itemsize for s in shapes)


def call(kernel, outs, args, scratch=(), smem=0, flops=0, space=VMEM, limit=32):
    return pl.pallas_call(
        kernel,
        out_shape=outs,
        in_specs=[SMEM] * smem + [space] * (len(args) - smem),
        out_specs=[VMEM] * len(outs),
        scratch_shapes=list(scratch),
        compiler_params=pltpu.CompilerParams(vmem_limit_bytes=limit * 1024 * 1024 if limit else None),
        cost_estimate=pl.CostEstimate(
            flops=flops, bytes_accessed=bytes_of(args) + bytes_of(outs), transcendentals=0
        ),
    )(*args)


def pack_kernel(swap, q, g, k, v, out, held, sems):
    half = BLK // 2
    copies = {}
    for place, ref in enumerate((q, g, k, v)):
        for part in range(2):
            rows = pl.ds(part * half, half)
            copies[place, part] = pltpu.make_async_copy(
                ref.at[0, rows], held.at[place, rows], sems.at[place, part]
            )
            copies[place, part].start()
    for (place, part), copy in copies.items():
        copy.wait()
        rows = slice(part * half, (part + 1) * half)
        lanes = slice((place % 2) * HD, (place % 2 + 1) * HD)
        for head in range(FRAMES):
            out[head ^ swap[0], place // 2, rows, lanes] = held[
                place, rows, head * HD : (head + 1) * HD
            ]


def unpack_kernel(swap, tile, dq, dk, dv):
    for place, ref in enumerate((dq, dk, dv)):
        for head in range(FRAMES):
            ref[0, :, head * HD : (head + 1) * HD] = tile[head ^ swap[0], place]


def block_diagonal(read, diag):
    diag[...] = jnp.zeros(diag.shape, BF)
    for f in range(FRAMES):
        both = read(f)
        diag[f, :BLK, :HD] = both[:, :HD]
        diag[f, BLK:, HD:] = both[:, HD:]


def wrap_frames(read, wrapped):
    for i in range(FRAMES + 2):
        wrapped[i * BLK : (i + 1) * BLK, :] = read((i - 1) % FRAMES)


def window(f):
    return slice(f * BLK, f * BLK + WIN)


def fold(tile):
    return tile.reshape(WIN // 8, 8, BLK)


def column_sums(columns, diag, f, before):
    both = [dot_nt(wrapped[window(f), :], diag[f]) for wrapped in columns]
    top8 = None
    for x in both:
        one = jnp.max(fold(x[:, :BLK]), axis=0)
        top8 = one if top8 is None else jnp.maximum(top8, one)
    top = jnp.max(top8, axis=0, keepdims=True) * EXP_SCALE
    if before is not None:
        top = jnp.maximum(top, before[0])
    total8 = jnp.zeros((8, BLK), F32)
    delta8 = jnp.zeros((8, BLK), F32)
    for x in both:
        e = jnp.exp2(x[:, :BLK] * EXP_SCALE - top)
        total8 = total8 + jnp.sum(fold(e), axis=0)
        delta8 = delta8 + jnp.sum(fold(e * x[:, BLK:]), axis=0)
    total = jnp.sum(total8, axis=0, keepdims=True)
    delta = jnp.sum(delta8, axis=0, keepdims=True)
    if before is not None:
        shrink = jnp.exp2(before[0] - top)
        total = total + before[1] * shrink
        delta = delta + before[2] * shrink
    return top, total, delta


def own_sums_kernel(tile, stats, queries, diag, kv_own):
    block_diagonal(lambda f: tile[f, 0], diag)
    wrap_frames(lambda f: tile[f, 1], kv_own)
    for f in range(FRAMES):
        queries[f] = tile[f, 0]
        for i, row in enumerate(column_sums((kv_own,), diag, f, None)):
            stats[i, f : f + 1, :] = row


def side_sums_kernel(tile, core, far, before, final, diag, kv_far, kv_core):
    block_diagonal(lambda f: tile[f, 0], diag)
    wrap_frames(lambda f: far[f], kv_far)
    wrap_frames(lambda f: core[f], kv_core)
    for f in range(FRAMES):
        rows = [before[i, f : f + 1, :] for i in range(3)]
        top, total, delta = column_sums((kv_far, kv_core), diag, f, rows)
        final[0, f : f + 1, :] = top + jnp.log2(total)
        final[1, f : f + 1, :] = delta / total


def prob_and_dscore(keys_values, diag, final, f):
    both = dot_nt(keys_values[window(f), :], diag[f])
    prob = jnp.exp2(both[:, :BLK] * EXP_SCALE - final[0, f : f + 1, :])
    dscore = prob * (both[:, BLK:] - final[1, f : f + 1, :])
    return prob.astype(BF), dscore.astype(BF)


def add_key_grads(dscore, prob, diag, f, total):
    both = jnp.concatenate([dscore, prob], axis=1)
    total[window(f), :] += dot_nn(both, diag[f])


def key_grads(total, u):
    got = total[(u + 1) * BLK : (u + 2) * BLK, :]
    if u == FRAMES - 1:
        got = got + total[:BLK, :]
    if u == 0:
        got = got + total[(FRAMES + 1) * BLK :, :]
    return got


def own_queries_kernel(
    tile, core, far, final, part, dq, diag, kv_own, kv_core, kv_far, kt, total
):
    columns = (kv_own, kv_core, kv_far)
    block_diagonal(lambda f: tile[f, 0], diag)
    wrap_frames(lambda f: tile[f, 1], kv_own)
    wrap_frames(lambda f: core[f], kv_core)
    wrap_frames(lambda f: far[f], kv_far)
    for j, wrapped in enumerate(columns):
        for i in range(FRAMES + 2):
            rows = slice(i * BLK, (i + 1) * BLK)
            kt[j, :, rows] = wrapped[rows, :HD].T
    total[...] = jnp.zeros(total.shape, F32)
    for f in range(FRAMES):
        acc = None
        for j, wrapped in enumerate(columns):
            prob, dscore = prob_and_dscore(wrapped, diag, final, f)
            one = dot_nn(kt[j, :, window(f)], dscore)
            acc = one if acc is None else acc + one
            if j == 0:
                add_key_grads(dscore, prob, diag, f, total)
        dq[f] = (acc * SCALE).T.astype(BF)
    for u in range(FRAMES):
        part[u] = key_grads(total, u)


def side_queries(tile, side, final, diag, kv_own, total):
    block_diagonal(lambda f: side[f], diag)
    wrap_frames(lambda f: tile[f, 1], kv_own)
    total[...] = jnp.zeros(total.shape, F32)
    for f in range(FRAMES):
        prob, dscore = prob_and_dscore(kv_own, diag, final, f)
        add_key_grads(dscore, prob, diag, f, total)


def core_queries_kernel(tile, side, final, before, part, diag, kv_own, total):
    side_queries(tile, side, final, diag, kv_own, total)
    for u in range(FRAMES):
        part[u] = before[u] + key_grads(total, u)


def far_queries_kernel(tile, side, final, before, dq, out, diag, kv_own, total):
    side_queries(tile, side, final, diag, kv_own, total)
    for u in range(FRAMES):
        both = before[u] + key_grads(total, u)
        out[u, 0] = dq[u]
        out[u, 1] = (both[:, :HD] * SCALE).astype(BF)
        out[u, 2] = both[:, HD:].astype(BF)


def on_device(queries, key_states, value_states, out_grad):
    swap = lax.axis_index("h").astype(jnp.int32).reshape(1)
    shape = jax.ShapeDtypeStruct
    both = (FRAMES, BLK, 2 * HD)
    wrapped = pltpu.VMEM(((FRAMES + 2) * BLK, 2 * HD), BF)
    summed = pltpu.VMEM(((FRAMES + 2) * BLK, 2 * HD), F32)
    diag = pltpu.VMEM((FRAMES, 2 * BLK, 2 * HD), BF)
    mats = 2 * BLK * BLK * HD * FRAMES * 3

    packed = call(
        pack_kernel,
        [shape((FRAMES, 2, BLK, 2 * HD), BF)],
        (swap, queries, out_grad, key_states, value_states),
        scratch=(pltpu.VMEM((4, BLK, FRAMES * HD), BF), pltpu.SemaphoreType.DMA((4, 2))),
        smem=1,
        space=HBM,
        limit=0,
    )[0]
    tile = lax.all_to_all(packed, ("x", "l"), 0, 0)
    keys_values = tile[:, 1]
    far_keys = move(keys_values, OVER_Z)
    core_keys = move(keys_values, CORE)
    sums, queries_grads = call(
        own_sums_kernel,
        [shape((3, FRAMES, BLK), F32), shape(both, BF)],
        (tile,),
        scratch=(diag, wrapped),
        flops=2 * mats,
    )
    far_queries = move(queries_grads, OVER_Z)
    core_queries = move(queries_grads, CORE)
    final = call(
        side_sums_kernel,
        [shape((2, FRAMES, BLK), F32)],
        (tile, core_keys, far_keys, sums),
        scratch=(diag, wrapped, wrapped),
        flops=4 * mats,
    )[0]
    far_final = move(final, OVER_Z)
    core_final = move(final, CORE)
    own_part, dq = call(
        own_queries_kernel,
        [shape(both, F32), shape((FRAMES, BLK, HD), BF)],
        (tile, core_keys, far_keys, final),
        scratch=(
            diag,
            wrapped,
            wrapped,
            wrapped,
            pltpu.VMEM((3, HD, (FRAMES + 2) * BLK), BF),
            summed,
        ),
        flops=11 * mats,
    )
    part = call(
        core_queries_kernel,
        [shape(both, F32)],
        (tile, core_queries, core_final, own_part),
        scratch=(diag, wrapped, summed),
        flops=4 * mats,
    )[0]
    grads = call(
        far_queries_kernel,
        [shape((FRAMES, 3, BLK, HD), BF)],
        (tile, far_queries, far_final, part, dq),
        scratch=(diag, wrapped, summed),
        flops=4 * mats,
    )[0]
    back = lax.all_to_all(grads, ("x", "l"), 0, 0)
    flat = shape((1, BLK, FRAMES * HD), BF)
    return tuple(call(unpack_kernel, [flat] * 3, (swap, back), smem=1))


def solution(mesh):
    fine = jax.sharding.Mesh(mesh.devices.reshape(SIZES), AXES)
    placed = P(("x", "l"), ("h", "z", "c"), None)
    return jax.shard_map(
        on_device,
        mesh=fine,
        in_specs=(placed,) * 4,
        out_specs=(placed,) * 3,
        check_vma=False,
    )
```

```python
import math

import jax
import jax.numpy as jnp
import numpy as np
from jax import lax
from jax.experimental import pallas as pl
from jax.experimental.pallas import tpu as pltpu
from jax.sharding import PartitionSpec as P

HD = 128
BLK = 128
FRAMES = 8
WIN = 3 * BLK
AXES = ("x", "l", "h", "z", "c")
SIZES = (4, 2, 2, 8, 2)
SCALE = 1.0 / math.sqrt(HD)
EXP_SCALE = SCALE * math.log2(math.e)
BF = jnp.bfloat16
F32 = jnp.float32
VMEM = pl.BlockSpec(memory_space=pltpu.VMEM)
HBM = pl.BlockSpec(memory_space=pltpu.HBM)
SMEM = pl.BlockSpec(memory_space=pltpu.SMEM)


def make_perm(target):
    pairs = []
    for index in range(math.prod(SIZES)):
        place = [int(v) for v in np.unravel_index(index, SIZES)]
        pairs.append((index, int(np.ravel_multi_index(target(*place), SIZES))))
    return pairs


def over_z(x, l, h, z, c):
    near = z + 2 * c - 1
    if 0 <= near < 8:
        return (x, l, h, near, 1 - c)
    return (x, 1 - l, 1 - h, near % 8, 1 - c)


CORE = make_perm(lambda x, l, h, z, c: (x, l, h, z, 1 - c))
OVER_Z = make_perm(over_z)


def move(value, perm):
    return lax.ppermute(value, AXES, perm)


def dot_nt(a, b):
    return lax.dot_general(a, b, (((1,), (1,)), ((), ())), preferred_element_type=F32)


def dot_nn(a, b):
    return lax.dot_general(a, b, (((1,), (0,)), ((), ())), preferred_element_type=F32)


def bytes_of(shapes):
    return sum(math.prod(s.shape) * s.dtype.itemsize for s in shapes)


def call(kernel, outs, args, scratch=(), smem=0, flops=0, space=VMEM, limit=32):
    return pl.pallas_call(
        kernel,
        out_shape=outs,
        in_specs=[SMEM] * smem + [space] * (len(args) - smem),
        out_specs=[VMEM] * len(outs),
        scratch_shapes=list(scratch),
        compiler_params=pltpu.CompilerParams(vmem_limit_bytes=limit * 1024 * 1024 if limit else None),
        cost_estimate=pl.CostEstimate(
            flops=flops, bytes_accessed=bytes_of(args) + bytes_of(outs), transcendentals=0
        ),
    )(*args)


def pack_kernel(swap, q, g, k, v, out, held, sems):
    half = BLK // 4
    copies = {}
    for place, ref in enumerate((q, g, k, v)):
        for part in range(4):
            rows = pl.ds(part * half, half)
            copies[place, part] = pltpu.make_async_copy(
                ref.at[0, rows], held.at[place, rows], sems.at[place, part]
            )
            copies[place, part].start()
    for (place, part), copy in copies.items():
        copy.wait()
        rows = slice(part * half, (part + 1) * half)
        lanes = slice((place % 2) * HD, (place % 2 + 1) * HD)
        for head in range(FRAMES):
            out[head ^ swap[0], place // 2, rows, lanes] = held[
                place, rows, head * HD : (head + 1) * HD
            ]


def unpack_kernel(swap, tile, dq, dk, dv):
    for place, ref in enumerate((dq, dk, dv)):
        for head in range(FRAMES):
            ref[0, :, head * HD : (head + 1) * HD] = tile[head ^ swap[0], place]


def block_diagonal(read, diag):
    diag[...] = jnp.zeros(diag.shape, BF)
    for f in range(FRAMES):
        both = read(f)
        diag[f, :BLK, :HD] = both[:, :HD]
        diag[f, BLK:, HD:] = both[:, HD:]


def wrap_frames(read, wrapped):
    for i in range(FRAMES + 2):
        wrapped[i * BLK : (i + 1) * BLK, :] = read((i - 1) % FRAMES)


def window(f):
    return slice(f * BLK, f * BLK + WIN)


def fold(tile):
    return tile.reshape(WIN // 8, 8, BLK)


def column_sums(columns, diag, f, before):
    both = [dot_nt(wrapped[window(f), :], diag[f]) for wrapped in columns]
    top8 = None
    for x in both:
        one = jnp.max(fold(x[:, :BLK]), axis=0)
        top8 = one if top8 is None else jnp.maximum(top8, one)
    top = jnp.max(top8, axis=0, keepdims=True) * EXP_SCALE
    if before is not None:
        top = jnp.maximum(top, before[0])
    total8 = jnp.zeros((8, BLK), F32)
    delta8 = jnp.zeros((8, BLK), F32)
    for x in both:
        e = jnp.exp2(x[:, :BLK] * EXP_SCALE - top)
        total8 = total8 + jnp.sum(fold(e), axis=0)
        delta8 = delta8 + jnp.sum(fold(e * x[:, BLK:]), axis=0)
    total = jnp.sum(total8, axis=0, keepdims=True)
    delta = jnp.sum(delta8, axis=0, keepdims=True)
    if before is not None:
        shrink = jnp.exp2(before[0] - top)
        total = total + before[1] * shrink
        delta = delta + before[2] * shrink
    return top, total, delta


def own_sums_kernel(tile, stats, queries, diag, kv_own):
    block_diagonal(lambda f: tile[f, 0], diag)
    wrap_frames(lambda f: tile[f, 1], kv_own)
    for f in range(FRAMES):
        queries[f] = tile[f, 0]
        for i, row in enumerate(column_sums((kv_own,), diag, f, None)):
            stats[i, f : f + 1, :] = row


def side_sums_kernel(tile, core, far, before, final, diag, kv_far, kv_core):
    block_diagonal(lambda f: tile[f, 0], diag)
    wrap_frames(lambda f: far[f], kv_far)
    wrap_frames(lambda f: core[f], kv_core)
    for f in range(FRAMES):
        rows = [before[i, f : f + 1, :] for i in range(3)]
        top, total, delta = column_sums((kv_far, kv_core), diag, f, rows)
        final[0, f : f + 1, :] = top + jnp.log2(total)
        final[1, f : f + 1, :] = delta / total


def prob_and_dscore(keys_values, diag, final, f):
    both = dot_nt(keys_values[window(f), :], diag[f])
    prob = jnp.exp2(both[:, :BLK] * EXP_SCALE - final[0, f : f + 1, :])
    dscore = prob * (both[:, BLK:] - final[1, f : f + 1, :])
    return prob.astype(BF), dscore.astype(BF)


def add_key_grads(dscore, prob, diag, f, total):
    both = jnp.concatenate([dscore, prob], axis=1)
    total[window(f), :] += dot_nn(both, diag[f])


def key_grads(total, u):
    got = total[(u + 1) * BLK : (u + 2) * BLK, :]
    if u == FRAMES - 1:
        got = got + total[:BLK, :]
    if u == 0:
        got = got + total[(FRAMES + 1) * BLK :, :]
    return got


def own_queries_kernel(
    tile, core, far, final, part, dq, diag, kv_own, kv_core, kv_far, kt, total
):
    columns = (kv_own, kv_core, kv_far)
    block_diagonal(lambda f: tile[f, 0], diag)
    wrap_frames(lambda f: tile[f, 1], kv_own)
    wrap_frames(lambda f: core[f], kv_core)
    wrap_frames(lambda f: far[f], kv_far)
    for j, wrapped in enumerate(columns):
        for i in range(FRAMES + 2):
            rows = slice(i * BLK, (i + 1) * BLK)
            kt[j, :, rows] = wrapped[rows, :HD].T
    total[...] = jnp.zeros(total.shape, F32)
    for f in range(FRAMES):
        acc = None
        for j, wrapped in enumerate(columns):
            prob, dscore = prob_and_dscore(wrapped, diag, final, f)
            one = dot_nn(kt[j, :, window(f)], dscore)
            acc = one if acc is None else acc + one
            if j == 0:
                add_key_grads(dscore, prob, diag, f, total)
        dq[f] = (acc * SCALE).T.astype(BF)
    for u in range(FRAMES):
        part[u] = key_grads(total, u)


def side_queries(tile, side, final, diag, kv_own, total):
    block_diagonal(lambda f: side[f], diag)
    wrap_frames(lambda f: tile[f, 1], kv_own)
    total[...] = jnp.zeros(total.shape, F32)
    for f in range(FRAMES):
        prob, dscore = prob_and_dscore(kv_own, diag, final, f)
        add_key_grads(dscore, prob, diag, f, total)


def core_queries_kernel(tile, side, final, before, part, diag, kv_own, total):
    side_queries(tile, side, final, diag, kv_own, total)
    for u in range(FRAMES):
        part[u] = before[u] + key_grads(total, u)


def far_queries_kernel(tile, side, final, before, dq, out, diag, kv_own, total):
    side_queries(tile, side, final, diag, kv_own, total)
    for u in range(FRAMES):
        both = before[u] + key_grads(total, u)
        out[u, 0] = dq[u]
        out[u, 1] = (both[:, :HD] * SCALE).astype(BF)
        out[u, 2] = both[:, HD:].astype(BF)


def on_device(queries, key_states, value_states, out_grad):
    swap = lax.axis_index("h").astype(jnp.int32).reshape(1)
    shape = jax.ShapeDtypeStruct
    both = (FRAMES, BLK, 2 * HD)
    wrapped = pltpu.VMEM(((FRAMES + 2) * BLK, 2 * HD), BF)
    summed = pltpu.VMEM(((FRAMES + 2) * BLK, 2 * HD), F32)
    diag = pltpu.VMEM((FRAMES, 2 * BLK, 2 * HD), BF)
    mats = 2 * BLK * BLK * HD * FRAMES * 3

    packed = call(
        pack_kernel,
        [pltpu.VMEM((FRAMES, 2, BLK, 2 * HD), BF)],
        (swap, queries, out_grad, key_states, value_states),
        scratch=(pltpu.VMEM((4, BLK, FRAMES * HD), BF), pltpu.SemaphoreType.DMA((4, 4))),
        smem=1,
        space=HBM,
        limit=0,
    )[0]
    tile = lax.all_to_all(packed, ("x", "l"), 0, 0)
    keys_values = tile[:, 1]
    far_keys = move(keys_values, OVER_Z)
    core_keys = move(keys_values, CORE)
    sums, queries_grads = call(
        own_sums_kernel,
        [shape((3, FRAMES, BLK), F32), shape(both, BF)],
        (tile,),
        scratch=(diag, wrapped),
        flops=2 * mats,
    )
    far_queries = move(queries_grads, OVER_Z)
    core_queries = move(queries_grads, CORE)
    final = call(
        side_sums_kernel,
        [shape((2, FRAMES, BLK), F32)],
        (tile, core_keys, far_keys, sums),
        scratch=(diag, wrapped, wrapped),
        flops=4 * mats,
    )[0]
    far_final = move(final, OVER_Z)
    core_final = move(final, CORE)
    own_part, dq = call(
        own_queries_kernel,
        [shape(both, F32), shape((FRAMES, BLK, HD), BF)],
        (tile, core_keys, far_keys, final),
        scratch=(
            diag,
            wrapped,
            wrapped,
            wrapped,
            pltpu.VMEM((3, HD, (FRAMES + 2) * BLK), BF),
            summed,
        ),
        flops=11 * mats,
    )
    part = call(
        core_queries_kernel,
        [shape(both, F32)],
        (tile, core_queries, core_final, own_part),
        scratch=(diag, wrapped, summed),
        flops=4 * mats,
    )[0]
    grads = call(
        far_queries_kernel,
        [shape((FRAMES, 3, BLK, HD), BF)],
        (tile, far_queries, far_final, part, dq),
        scratch=(diag, wrapped, summed),
        flops=4 * mats,
    )[0]
    back = lax.all_to_all(grads, ("x", "l"), 0, 0)
    flat = shape((1, BLK, FRAMES * HD), BF)
    return tuple(call(unpack_kernel, [flat] * 3, (swap, back), smem=1))


def solution(mesh):
    fine = jax.sharding.Mesh(mesh.devices.reshape(SIZES), AXES)
    placed = P(("x", "l"), ("h", "z", "c"), None)
    return jax.shard_map(
        on_device,
        mesh=fine,
        in_specs=(placed,) * 4,
        out_specs=(placed,) * 3,
        check_vma=False,
    )
```

```python
import math

import jax
import jax.numpy as jnp
import numpy as np
from jax import lax
from jax.experimental import pallas as pl
from jax.experimental.pallas import tpu as pltpu
from jax.sharding import PartitionSpec as P

HD = 128
BLK = 128
FRAMES = 8
WIN = 3 * BLK
AXES = ("x", "l", "h", "z", "c")
SIZES = (4, 2, 2, 8, 2)
SCALE = 1.0 / math.sqrt(HD)
EXP_SCALE = SCALE * math.log2(math.e)
BF = jnp.bfloat16
F32 = jnp.float32
VMEM = pl.BlockSpec(memory_space=pltpu.VMEM)
HBM = pl.BlockSpec(memory_space=pltpu.HBM)
SMEM = pl.BlockSpec(memory_space=pltpu.SMEM)


def make_perm(target):
    pairs = []
    for index in range(math.prod(SIZES)):
        place = [int(v) for v in np.unravel_index(index, SIZES)]
        pairs.append((index, int(np.ravel_multi_index(target(*place), SIZES))))
    return pairs


def over_z(x, l, h, z, c):
    near = z + 2 * c - 1
    if 0 <= near < 8:
        return (x, l, h, near, 1 - c)
    return (x, 1 - l, 1 - h, near % 8, 1 - c)


CORE = make_perm(lambda x, l, h, z, c: (x, l, h, z, 1 - c))
OVER_Z = make_perm(over_z)


def move(value, perm):
    return lax.ppermute(value, AXES, perm)


def dot_nt(a, b):
    return lax.dot_general(a, b, (((1,), (1,)), ((), ())), preferred_element_type=F32)


def dot_nn(a, b):
    return lax.dot_general(a, b, (((1,), (0,)), ((), ())), preferred_element_type=F32)


def bytes_of(shapes):
    return sum(math.prod(s.shape) * s.dtype.itemsize for s in shapes)


def call(kernel, outs, args, scratch=(), smem=0, flops=0, space=VMEM, limit=32):
    return pl.pallas_call(
        kernel,
        out_shape=outs,
        in_specs=[SMEM] * smem + [space] * (len(args) - smem),
        out_specs=[VMEM] * len(outs),
        scratch_shapes=list(scratch),
        compiler_params=pltpu.CompilerParams(vmem_limit_bytes=limit * 1024 * 1024 if limit else None),
        cost_estimate=pl.CostEstimate(
            flops=flops, bytes_accessed=bytes_of(args) + bytes_of(outs), transcendentals=0
        ),
    )(*args)


def pack_kernel(swap, q, g, k, v, out, held, sems):
    half = BLK // 4
    copies = {}
    for place, ref in enumerate((q, g, k, v)):
        for part in range(4):
            rows = pl.ds(part * half, half)
            copies[place, part] = pltpu.make_async_copy(
                ref.at[0, rows], held.at[place, rows], sems.at[place, part]
            )
            copies[place, part].start()
    for (place, part), copy in copies.items():
        copy.wait()
        rows = slice(part * half, (part + 1) * half)
        lanes = slice((place % 2) * HD, (place % 2 + 1) * HD)
        for head in range(FRAMES):
            out[head ^ swap[0], place // 2, rows, lanes] = held[
                place, rows, head * HD : (head + 1) * HD
            ]


def unpack_kernel(swap, tile, dq, dk, dv):
    for place, ref in enumerate((dq, dk, dv)):
        for head in range(FRAMES):
            ref[0, :, head * HD : (head + 1) * HD] = tile[head ^ swap[0], place]


def block_diagonal(read, diag):
    diag[...] = jnp.zeros(diag.shape, BF)
    for f in range(FRAMES):
        both = read(f)
        diag[f, :BLK, :HD] = both[:, :HD]
        diag[f, BLK:, HD:] = both[:, HD:]


def wrap_frames(read, wrapped):
    for i in range(FRAMES + 2):
        wrapped[i * BLK : (i + 1) * BLK, :] = read((i - 1) % FRAMES)


def window(f):
    return slice(f * BLK, f * BLK + WIN)


def fold(tile):
    return tile.reshape(WIN // 8, 8, BLK)


def column_sums(columns, diag, f, before):
    both = [dot_nt(wrapped[window(f), :], diag[f]) for wrapped in columns]
    top8 = None
    for x in both:
        one = jnp.max(fold(x[:, :BLK]), axis=0)
        top8 = one if top8 is None else jnp.maximum(top8, one)
    top = jnp.max(top8, axis=0, keepdims=True) * EXP_SCALE
    if before is not None:
        top = jnp.maximum(top, before[0])
    total8 = jnp.zeros((8, BLK), F32)
    delta8 = jnp.zeros((8, BLK), F32)
    for x in both:
        e = jnp.exp2(x[:, :BLK] * EXP_SCALE - top)
        total8 = total8 + jnp.sum(fold(e), axis=0)
        delta8 = delta8 + jnp.sum(fold(e * x[:, BLK:]), axis=0)
    total = jnp.sum(total8, axis=0, keepdims=True)
    delta = jnp.sum(delta8, axis=0, keepdims=True)
    if before is not None:
        shrink = jnp.exp2(before[0] - top)
        total = total + before[1] * shrink
        delta = delta + before[2] * shrink
    return top, total, delta


def own_sums_kernel(tile, stats, queries, diag, kv_own, kt_own):
    block_diagonal(lambda f: tile[f, 0], diag)
    wrap_frames(lambda f: tile[f, 1], kv_own)
    for i in range(FRAMES + 2):
        rows = slice(i * BLK, (i + 1) * BLK)
        kt_own[:, rows] = kv_own[rows, :HD].T
    for f in range(FRAMES):
        queries[f] = tile[f, 0]
        for i, row in enumerate(column_sums((kv_own,), diag, f, None)):
            stats[i, f : f + 1, :] = row


def side_sums_kernel(diag, far, core, before, final, kv_far, kv_core):
    wrap_frames(lambda f: far[f], kv_far)
    wrap_frames(lambda f: core[f], kv_core)
    for f in range(FRAMES):
        rows = [before[i, f : f + 1, :] for i in range(3)]
        top, total, delta = column_sums((kv_far, kv_core), diag, f, rows)
        final[0, f : f + 1, :] = top + jnp.log2(total)
        final[1, f : f + 1, :] = delta / total


def prob_and_dscore(keys_values, diag, final, f):
    both = dot_nt(keys_values[window(f), :], diag[f])
    prob = jnp.exp2(both[:, :BLK] * EXP_SCALE - final[0, f : f + 1, :])
    dscore = prob * (both[:, BLK:] - final[1, f : f + 1, :])
    return prob.astype(BF), dscore.astype(BF)


def add_key_grads(dscore, prob, diag, f, total):
    both = jnp.concatenate([dscore, prob], axis=1)
    total[window(f), :] += dot_nn(both, diag[f])


def key_grads(total, u):
    got = total[(u + 1) * BLK : (u + 2) * BLK, :]
    if u == FRAMES - 1:
        got = got + total[:BLK, :]
    if u == 0:
        got = got + total[(FRAMES + 1) * BLK :, :]
    return got


def near_queries_kernel(
    diag, kv_own, kt_own, core, far, final, side, side_final, part, dq,
    side_diag, kv_core, kv_far, kt, total,
):
    columns = (kv_own, kv_core, kv_far)
    block_diagonal(lambda f: side[f], side_diag)
    wrap_frames(lambda f: core[f], kv_core)
    wrap_frames(lambda f: far[f], kv_far)
    turned = (kt_own, kt.at[0], kt.at[1])
    for keys, wrapped in zip(turned[1:], columns[1:]):
        for i in range(FRAMES + 2):
            rows = slice(i * BLK, (i + 1) * BLK)
            keys[:, rows] = wrapped[rows, :HD].T
    total[...] = jnp.zeros(total.shape, F32)
    for f in range(FRAMES):
        acc = None
        for j, wrapped in enumerate(columns):
            prob, dscore = prob_and_dscore(wrapped, diag, final, f)
            one = dot_nn(turned[j][:, window(f)], dscore)
            acc = one if acc is None else acc + one
            if j == 0:
                add_key_grads(dscore, prob, diag, f, total)
        dq[f] = (acc * SCALE).T.astype(BF)
        prob, dscore = prob_and_dscore(kv_own, side_diag, side_final, f)
        add_key_grads(dscore, prob, side_diag, f, total)
    for u in range(FRAMES):
        part[u] = key_grads(total, u)


def far_queries_kernel(kv_own, side, final, before, dq, out, diag, total):
    block_diagonal(lambda f: side[f], diag)
    total[...] = jnp.zeros(total.shape, F32)
    for f in range(FRAMES):
        prob, dscore = prob_and_dscore(kv_own, diag, final, f)
        add_key_grads(dscore, prob, diag, f, total)
    for u in range(FRAMES):
        both = before[u] + key_grads(total, u)
        out[u, 0] = dq[u]
        out[u, 1] = (both[:, :HD] * SCALE).astype(BF)
        out[u, 2] = both[:, HD:].astype(BF)


def on_device(queries, key_states, value_states, out_grad):
    swap = lax.axis_index("h").astype(jnp.int32).reshape(1)
    shape = jax.ShapeDtypeStruct
    both = (FRAMES, BLK, 2 * HD)
    wrapped = pltpu.VMEM(((FRAMES + 2) * BLK, 2 * HD), BF)
    summed = pltpu.VMEM(((FRAMES + 2) * BLK, 2 * HD), F32)
    diag = pltpu.VMEM((FRAMES, 2 * BLK, 2 * HD), BF)
    mats = 2 * BLK * BLK * HD * FRAMES * 3

    packed = call(
        pack_kernel,
        [pltpu.VMEM((FRAMES, 2, BLK, 2 * HD), BF)],
        (swap, queries, out_grad, key_states, value_states),
        scratch=(pltpu.VMEM((4, BLK, FRAMES * HD), BF), pltpu.SemaphoreType.DMA((4, 4))),
        smem=1,
        space=HBM,
        limit=0,
    )[0]
    tile = lax.all_to_all(packed, ("x", "l"), 0, 0)
    keys_values = tile[:, 1]
    far_keys = move(keys_values, OVER_Z)
    core_keys = move(keys_values, CORE)
    sums, queries_grads, own_diag, own_wrap, own_kt = call(
        own_sums_kernel,
        [
            shape((3, FRAMES, BLK), F32),
            shape(both, BF),
            shape((FRAMES, 2 * BLK, 2 * HD), BF),
            shape(((FRAMES + 2) * BLK, 2 * HD), BF),
            shape((HD, (FRAMES + 2) * BLK), BF),
        ],
        (tile,),
        flops=2 * mats,
    )
    far_queries = move(queries_grads, OVER_Z)
    core_queries = move(queries_grads, CORE)
    final = call(
        side_sums_kernel,
        [shape((2, FRAMES, BLK), F32)],
        (own_diag, far_keys, core_keys, sums),
        scratch=(wrapped, wrapped),
        flops=4 * mats,
    )[0]
    far_final = move(final, OVER_Z)
    core_final = move(final, CORE)
    part, dq = call(
        near_queries_kernel,
        [shape(both, F32), shape((FRAMES, BLK, HD), BF)],
        (own_diag, own_wrap, own_kt, core_keys, far_keys, final, core_queries, core_final),
        scratch=(
            diag,
            wrapped,
            wrapped,
            pltpu.VMEM((2, HD, (FRAMES + 2) * BLK), BF),
            summed,
        ),
        flops=15 * mats,
    )
    grads = call(
        far_queries_kernel,
        [shape((FRAMES, 3, BLK, HD), BF)],
        (own_wrap, far_queries, far_final, part, dq),
        scratch=(diag, summed),
        flops=4 * mats,
    )[0]
    back = lax.all_to_all(grads, ("x", "l"), 0, 0)
    flat = shape((1, BLK, FRAMES * HD), BF)
    return tuple(call(unpack_kernel, [flat] * 3, (swap, back), smem=1))


def solution(mesh):
    fine = jax.sharding.Mesh(mesh.devices.reshape(SIZES), AXES)
    placed = P(("x", "l"), ("h", "z", "c"), None)
    return jax.shard_map(
        on_device,
        mesh=fine,
        in_specs=(placed,) * 4,
        out_specs=(placed,) * 3,
        check_vma=False,
    )
```

```python
import math

import jax
import jax.numpy as jnp
import numpy as np
from jax import lax
from jax.experimental import pallas as pl
from jax.experimental.pallas import tpu as pltpu
from jax.sharding import PartitionSpec as P

HD = 128
BLK = 128
FRAMES = 8
WIN = 3 * BLK
AXES = ("x", "l", "h", "z", "c")
SIZES = (4, 2, 2, 8, 2)
SCALE = 1.0 / math.sqrt(HD)
EXP_SCALE = SCALE * math.log2(math.e)
BF = jnp.bfloat16
F32 = jnp.float32
VMEM = pl.BlockSpec(memory_space=pltpu.VMEM)
HBM = pl.BlockSpec(memory_space=pltpu.HBM)
SMEM = pl.BlockSpec(memory_space=pltpu.SMEM)


def make_perm(target):
    pairs = []
    for index in range(math.prod(SIZES)):
        place = [int(v) for v in np.unravel_index(index, SIZES)]
        pairs.append((index, int(np.ravel_multi_index(target(*place), SIZES))))
    return pairs


def over_z(x, l, h, z, c):
    near = z + 2 * c - 1
    if 0 <= near < 8:
        return (x, l, h, near, 1 - c)
    return (x, 1 - l, 1 - h, near % 8, 1 - c)


CORE = make_perm(lambda x, l, h, z, c: (x, l, h, z, 1 - c))
OVER_Z = make_perm(over_z)


def move(value, perm):
    return lax.ppermute(value, AXES, perm)


def dot_nt(a, b):
    return lax.dot_general(a, b, (((1,), (1,)), ((), ())), preferred_element_type=F32)


def dot_nn(a, b):
    return lax.dot_general(a, b, (((1,), (0,)), ((), ())), preferred_element_type=F32)


def bytes_of(shapes):
    return sum(math.prod(s.shape) * s.dtype.itemsize for s in shapes)


def call(kernel, outs, args, scratch=(), smem=0, flops=0, space=VMEM, limit=32, out_space=VMEM):
    return pl.pallas_call(
        kernel,
        out_shape=outs,
        in_specs=[SMEM] * smem + [space] * (len(args) - smem),
        out_specs=[out_space] * len(outs),
        scratch_shapes=list(scratch),
        compiler_params=pltpu.CompilerParams(vmem_limit_bytes=limit * 1024 * 1024 if limit else None),
        cost_estimate=pl.CostEstimate(
            flops=flops, bytes_accessed=bytes_of(args) + bytes_of(outs), transcendentals=0
        ),
    )(*args)


def pack_kernel(swap, q, g, k, v, out, held, sems):
    half = BLK // 4
    copies = {}
    for place, ref in enumerate((q, g, k, v)):
        for part in range(4):
            rows = pl.ds(part * half, half)
            copies[place, part] = pltpu.make_async_copy(
                ref.at[0, rows], held.at[place, rows], sems.at[place, part]
            )
            copies[place, part].start()
    for (place, part), copy in copies.items():
        copy.wait()
        rows = slice(part * half, (part + 1) * half)
        lanes = slice((place % 2) * HD, (place % 2 + 1) * HD)
        for head in range(FRAMES):
            out[head ^ swap[0], place // 2, rows, lanes] = held[
                place, rows, head * HD : (head + 1) * HD
            ]


def unpack_kernel(swap, tile, dq, dk, dv, held, sems):
    step = BLK // 4
    copies = []
    for place, ref in enumerate((dq, dk, dv)):
        for part in range(4):
            rows = slice(part * step, (part + 1) * step)
            for head in range(FRAMES):
                lanes = slice(head * HD, (head + 1) * HD)
                held[place, rows, lanes] = tile[head ^ swap[0], place, rows]
            span = pl.ds(part * step, step)
            copy = pltpu.make_async_copy(
                held.at[place, span], ref.at[0, span], sems.at[place, part]
            )
            copy.start()
            copies.append(copy)
    for copy in copies:
        copy.wait()


def block_diagonal(read, diag):
    diag[...] = jnp.zeros(diag.shape, BF)
    for f in range(FRAMES):
        both = read(f)
        diag[f, :BLK, :HD] = both[:, :HD]
        diag[f, BLK:, HD:] = both[:, HD:]


def wrap_frames(read, wrapped):
    for i in range(FRAMES + 2):
        wrapped[i * BLK : (i + 1) * BLK, :] = read((i - 1) % FRAMES)


def window(f):
    return slice(f * BLK, f * BLK + WIN)


def fold(tile):
    return tile.reshape(WIN // 8, 8, BLK)


def column_sums(columns, diag, f, before):
    for wrapped in columns:
        x = dot_nt(wrapped[window(f), :], diag[f])
        top = jnp.max(jnp.max(fold(x[:, :BLK]), axis=0), axis=0, keepdims=True) * EXP_SCALE
        if before is not None:
            top = jnp.maximum(top, before[0])
        e = jnp.exp2(x[:, :BLK] * EXP_SCALE - top)
        total = jnp.sum(jnp.sum(fold(e), axis=0), axis=0, keepdims=True)
        delta = jnp.sum(jnp.sum(fold(e * x[:, BLK:]), axis=0), axis=0, keepdims=True)
        if before is not None:
            shrink = jnp.exp2(before[0] - top)
            total = total + before[1] * shrink
            delta = delta + before[2] * shrink
        before = (top, total, delta)
    return before


def own_sums_kernel(tile, stats, queries, diag, kv_own, kt_own):
    block_diagonal(lambda f: tile[f, 0], diag)
    wrap_frames(lambda f: tile[f, 1], kv_own)
    for i in range(FRAMES + 2):
        rows = slice(i * BLK, (i + 1) * BLK)
        kt_own[:, rows] = kv_own[rows, :HD].T
    for f in range(FRAMES):
        queries[f] = tile[f, 0]
        for i, row in enumerate(column_sums((kv_own,), diag, f, None)):
            stats[i, f : f + 1, :] = row


def side_sums_kernel(diag, far, core, before, final, kv_far, kv_core):
    wrap_frames(lambda f: far[f], kv_far)
    wrap_frames(lambda f: core[f], kv_core)
    for f in range(FRAMES):
        rows = [before[i, f : f + 1, :] for i in range(3)]
        top, total, delta = column_sums((kv_far, kv_core), diag, f, rows)
        final[0, f : f + 1, :] = top + jnp.log2(total)
        final[1, f : f + 1, :] = delta / total


def prob_and_dscore(keys_values, diag, final, f):
    both = dot_nt(keys_values[window(f), :], diag[f])
    prob = jnp.exp2(both[:, :BLK] * EXP_SCALE - final[0, f : f + 1, :])
    dscore = prob * (both[:, BLK:] - final[1, f : f + 1, :])
    return prob.astype(BF), dscore.astype(BF)


def add_key_grads(dscore, prob, diag, f, total):
    both = jnp.concatenate([dscore, prob], axis=1)
    total[window(f), :] += dot_nn(both, diag[f])


def key_grads(total, u):
    got = total[(u + 1) * BLK : (u + 2) * BLK, :]
    if u == FRAMES - 1:
        got = got + total[:BLK, :]
    if u == 0:
        got = got + total[(FRAMES + 1) * BLK :, :]
    return got


def near_queries_kernel(
    diag, kv_own, kt_own, core, far, final, side, side_final, part, dq,
    side_diag, kv_core, kv_far, kt, total,
):
    columns = (kv_own, kv_core, kv_far)
    block_diagonal(lambda f: side[f], side_diag)
    wrap_frames(lambda f: core[f], kv_core)
    wrap_frames(lambda f: far[f], kv_far)
    turned = (kt_own, kt.at[0], kt.at[1])
    for keys, wrapped in zip(turned[1:], columns[1:]):
        for i in range(FRAMES + 2):
            rows = slice(i * BLK, (i + 1) * BLK)
            keys[:, rows] = wrapped[rows, :HD].T
    total[...] = jnp.zeros(total.shape, F32)
    for f in range(FRAMES):
        acc = None
        for j, wrapped in enumerate(columns):
            prob, dscore = prob_and_dscore(wrapped, diag, final, f)
            one = dot_nn(turned[j][:, window(f)], dscore)
            acc = one if acc is None else acc + one
            if j == 0:
                add_key_grads(dscore, prob, diag, f, total)
        dq[f] = (acc * SCALE).T.astype(BF)
        prob, dscore = prob_and_dscore(kv_own, side_diag, side_final, f)
        add_key_grads(dscore, prob, side_diag, f, total)
    for u in range(FRAMES):
        part[u] = key_grads(total, u)


def far_queries_kernel(kv_own, side, final, before, dq, out, diag, total):
    block_diagonal(lambda f: side[f], diag)
    total[...] = jnp.zeros(total.shape, F32)
    for f in range(FRAMES):
        prob, dscore = prob_and_dscore(kv_own, diag, final, f)
        add_key_grads(dscore, prob, diag, f, total)
    for u in range(FRAMES):
        both = before[u] + key_grads(total, u)
        out[u, 0] = dq[u]
        out[u, 1] = (both[:, :HD] * SCALE).astype(BF)
        out[u, 2] = both[:, HD:].astype(BF)


def on_device(queries, key_states, value_states, out_grad):
    swap = lax.axis_index("h").astype(jnp.int32).reshape(1)
    shape = jax.ShapeDtypeStruct
    both = (FRAMES, BLK, 2 * HD)
    wrapped = pltpu.VMEM(((FRAMES + 2) * BLK, 2 * HD), BF)
    summed = pltpu.VMEM(((FRAMES + 2) * BLK, 2 * HD), F32)
    diag = pltpu.VMEM((FRAMES, 2 * BLK, 2 * HD), BF)
    mats = 2 * BLK * BLK * HD * FRAMES * 3

    packed = call(
        pack_kernel,
        [pltpu.VMEM((FRAMES, 2, BLK, 2 * HD), BF)],
        (swap, queries, out_grad, key_states, value_states),
        scratch=(pltpu.VMEM((4, BLK, FRAMES * HD), BF), pltpu.SemaphoreType.DMA((4, 4))),
        smem=1,
        space=HBM,
        limit=0,
    )[0]
    tile = lax.all_to_all(packed, ("x", "l"), 0, 0)
    keys_values = tile[:, 1]
    far_keys = move(keys_values, OVER_Z)
    core_keys = move(keys_values, CORE)
    sums, queries_grads, own_diag, own_wrap, own_kt = call(
        own_sums_kernel,
        [
            shape((3, FRAMES, BLK), F32),
            shape(both, BF),
            shape((FRAMES, 2 * BLK, 2 * HD), BF),
            shape(((FRAMES + 2) * BLK, 2 * HD), BF),
            shape((HD, (FRAMES + 2) * BLK), BF),
        ],
        (tile,),
        flops=2 * mats,
    )
    far_queries = move(queries_grads, OVER_Z)
    core_queries = move(queries_grads, CORE)
    final = call(
        side_sums_kernel,
        [shape((2, FRAMES, BLK), F32)],
        (own_diag, far_keys, core_keys, sums),
        scratch=(wrapped, wrapped),
        flops=4 * mats,
    )[0]
    far_final = move(final, OVER_Z)
    core_final = move(final, CORE)
    part, dq = call(
        near_queries_kernel,
        [shape(both, F32), shape((FRAMES, BLK, HD), BF)],
        (own_diag, own_wrap, own_kt, core_keys, far_keys, final, core_queries, core_final),
        scratch=(
            diag,
            wrapped,
            wrapped,
            pltpu.VMEM((2, HD, (FRAMES + 2) * BLK), BF),
            summed,
        ),
        flops=15 * mats,
    )
    grads = call(
        far_queries_kernel,
        [shape((FRAMES, 3, BLK, HD), BF)],
        (own_wrap, far_queries, far_final, part, dq),
        scratch=(diag, summed),
        flops=4 * mats,
    )[0]
    back = lax.all_to_all(grads, ("x", "l"), 0, 0)
    flat = shape((1, BLK, FRAMES * HD), BF)
    return tuple(
        call(
            unpack_kernel,
            [flat] * 3,
            (swap, back),
            scratch=(pltpu.VMEM((3, BLK, FRAMES * HD), BF), pltpu.SemaphoreType.DMA((3, 4))),
            smem=1,
            out_space=HBM,
        )
    )


def solution(mesh):
    fine = jax.sharding.Mesh(mesh.devices.reshape(SIZES), AXES)
    placed = P(("x", "l"), ("h", "z", "c"), None)
    return jax.shard_map(
        on_device,
        mesh=fine,
        in_specs=(placed,) * 4,
        out_specs=(placed,) * 3,
        check_vma=False,
    )
```

```python
import math

import jax
import jax.numpy as jnp
import numpy as np
from jax import lax
from jax.experimental import pallas as pl
from jax.experimental.pallas import tpu as pltpu
from jax.sharding import PartitionSpec as P

HD = 128
BLK = 128
FRAMES = 8
WIN = 3 * BLK
AXES = ("x", "l", "h", "z", "c")
SIZES = (4, 2, 2, 8, 2)
SCALE = 1.0 / math.sqrt(HD)
EXP_SCALE = SCALE * math.log2(math.e)
BF = jnp.bfloat16
F32 = jnp.float32
VMEM = pl.BlockSpec(memory_space=pltpu.VMEM)
HBM = pl.BlockSpec(memory_space=pltpu.HBM)
SMEM = pl.BlockSpec(memory_space=pltpu.SMEM)


def make_perm(target):
    pairs = []
    for index in range(math.prod(SIZES)):
        place = [int(v) for v in np.unravel_index(index, SIZES)]
        pairs.append((index, int(np.ravel_multi_index(target(*place), SIZES))))
    return pairs


def over_z(x, l, h, z, c):
    near = z + 2 * c - 1
    if 0 <= near < 8:
        return (x, l, h, near, 1 - c)
    return (x, 1 - l, 1 - h, near % 8, 1 - c)


CORE = make_perm(lambda x, l, h, z, c: (x, l, h, z, 1 - c))
OVER_Z = make_perm(over_z)


def move(value, perm):
    return lax.ppermute(value, AXES, perm)


def dot_nt(a, b):
    return lax.dot_general(a, b, (((1,), (1,)), ((), ())), preferred_element_type=F32)


def dot_nn(a, b):
    return lax.dot_general(a, b, (((1,), (0,)), ((), ())), preferred_element_type=F32)


def bytes_of(shapes):
    return sum(math.prod(s.shape) * s.dtype.itemsize for s in shapes)


def call(kernel, outs, args, scratch=(), smem=0, flops=0, space=VMEM, limit=32, out_space=VMEM):
    return pl.pallas_call(
        kernel,
        out_shape=outs,
        in_specs=[SMEM] * smem + [space] * (len(args) - smem),
        out_specs=[out_space] * len(outs),
        scratch_shapes=list(scratch),
        compiler_params=pltpu.CompilerParams(vmem_limit_bytes=limit * 1024 * 1024 if limit else None),
        cost_estimate=pl.CostEstimate(
            flops=flops, bytes_accessed=bytes_of(args) + bytes_of(outs), transcendentals=0
        ),
    )(*args)


def pack_kernel(swap, q, g, k, v, out, held, sems):
    half = BLK // 4
    copies = {}
    for place, ref in enumerate((q, g, k, v)):
        for part in range(4):
            rows = pl.ds(part * half, half)
            copies[place, part] = pltpu.make_async_copy(
                ref.at[0, rows], held.at[place, rows], sems.at[place, part]
            )
            copies[place, part].start()
    for (place, part), copy in copies.items():
        copy.wait()
        rows = slice(part * half, (part + 1) * half)
        lanes = slice((place % 2) * HD, (place % 2 + 1) * HD)
        for head in range(FRAMES):
            out[head ^ swap[0], place // 2, rows, lanes] = held[
                place, rows, head * HD : (head + 1) * HD
            ]


def unpack_kernel(swap, tile, dq, dk, dv, held, sems):
    step = BLK // 4
    copies = []
    for place, ref in enumerate((dq, dk, dv)):
        for part in range(4):
            rows = slice(part * step, (part + 1) * step)
            for head in range(FRAMES):
                lanes = slice(head * HD, (head + 1) * HD)
                held[place, rows, lanes] = tile[head ^ swap[0], place, rows]
            span = pl.ds(part * step, step)
            copy = pltpu.make_async_copy(
                held.at[place, span], ref.at[0, span], sems.at[place, part]
            )
            copy.start()
            copies.append(copy)
    for copy in copies:
        copy.wait()


def block_diagonal(read, diag):
    diag[...] = jnp.zeros(diag.shape, BF)
    for f in range(FRAMES):
        both = read(f)
        diag[f, :BLK, :HD] = both[:, :HD]
        diag[f, BLK:, HD:] = both[:, HD:]


def wrap_frames(read, wrapped):
    for i in range(FRAMES + 2):
        wrapped[i * BLK : (i + 1) * BLK, :] = read((i - 1) % FRAMES)


def window(f):
    return slice(f * BLK, f * BLK + WIN)


def fold(tile):
    return tile.reshape(WIN // 8, 8, BLK)


def column_sums(columns, diag, f, before):
    for wrapped in columns:
        x = dot_nt(wrapped[window(f), :], diag[f])
        top = jnp.max(jnp.max(fold(x[:, :BLK]), axis=0), axis=0, keepdims=True) * EXP_SCALE
        if before is not None:
            top = jnp.maximum(top, before[0])
        e = jnp.exp2(x[:, :BLK] * EXP_SCALE - top)
        total = jnp.sum(jnp.sum(fold(e), axis=0), axis=0, keepdims=True)
        delta = jnp.sum(jnp.sum(fold(e * x[:, BLK:]), axis=0), axis=0, keepdims=True)
        if before is not None:
            shrink = jnp.exp2(before[0] - top)
            total = total + before[1] * shrink
            delta = delta + before[2] * shrink
        before = (top, total, delta)
    return before


def own_sums_kernel(tile, stats, queries, diag, kv_own, kt_own):
    block_diagonal(lambda f: tile[f, 0], diag)
    wrap_frames(lambda f: tile[f, 1], kv_own)
    for i in range(FRAMES + 2):
        rows = slice(i * BLK, (i + 1) * BLK)
        kt_own[:, rows] = kv_own[rows, :HD].T
    for f in range(FRAMES):
        queries[f] = tile[f, 0]
        for i, row in enumerate(column_sums((kv_own,), diag, f, None)):
            stats[i, f : f + 1, :] = row


def side_sums_kernel(diag, far, core, before, final, kv_far, kv_core):
    wrap_frames(lambda f: far[f], kv_far)
    wrap_frames(lambda f: core[f], kv_core)
    for f in range(FRAMES):
        rows = [before[i, f : f + 1, :] for i in range(3)]
        top, total, delta = column_sums((kv_far, kv_core), diag, f, rows)
        final[0, f : f + 1, :] = top + jnp.log2(total)
        final[1, f : f + 1, :] = delta / total


def prob_and_dscore(keys_values, diag, final, f):
    both = dot_nt(keys_values[window(f), :], diag[f])
    prob = jnp.exp2(both[:, :BLK] * EXP_SCALE - final[0, f : f + 1, :])
    dscore = prob * (both[:, BLK:] - final[1, f : f + 1, :])
    return prob.astype(BF), dscore.astype(BF)


def add_key_grads(dscore, prob, diag, f, total, fresh):
    got = dot_nn(jnp.concatenate([dscore, prob], axis=1), diag[f])
    old = 0 if fresh and f == 0 else 2 * BLK if fresh else WIN
    start = f * BLK
    if old:
        total[start : start + old, :] += got[:old, :]
    if old < WIN:
        total[start + old : start + WIN, :] = got[old:, :]


def key_grads(total, u):
    got = total[(u + 1) * BLK : (u + 2) * BLK, :]
    if u == FRAMES - 1:
        got = got + total[:BLK, :]
    if u == 0:
        got = got + total[(FRAMES + 1) * BLK :, :]
    return got


def near_queries_kernel(
    diag, kv_own, kt_own, core, far, final, side, side_final, part, dq,
    side_diag, kv_core, kv_far, kt, total,
):
    columns = (kv_own, kv_core, kv_far)
    block_diagonal(lambda f: side[f], side_diag)
    wrap_frames(lambda f: core[f], kv_core)
    wrap_frames(lambda f: far[f], kv_far)
    turned = (kt_own, kt.at[0], kt.at[1])
    for keys, wrapped in zip(turned[1:], columns[1:]):
        for i in range(FRAMES + 2):
            rows = slice(i * BLK, (i + 1) * BLK)
            keys[:, rows] = wrapped[rows, :HD].T
    for f in range(FRAMES):
        acc = None
        for j, wrapped in enumerate(columns):
            prob, dscore = prob_and_dscore(wrapped, diag, final, f)
            one = dot_nn(turned[j][:, window(f)], dscore)
            acc = one if acc is None else acc + one
            if j == 0:
                add_key_grads(dscore, prob, diag, f, total, True)
        dq[f] = (acc * SCALE).T.astype(BF)
        prob, dscore = prob_and_dscore(kv_own, side_diag, side_final, f)
        add_key_grads(dscore, prob, side_diag, f, total, False)
    for u in range(FRAMES):
        part[u] = key_grads(total, u)


def far_queries_kernel(kv_own, side, final, before, dq, out, diag, total):
    block_diagonal(lambda f: side[f], diag)
    for f in range(FRAMES):
        prob, dscore = prob_and_dscore(kv_own, diag, final, f)
        add_key_grads(dscore, prob, diag, f, total, True)
    for u in range(FRAMES):
        both = before[u] + key_grads(total, u)
        out[u, 0] = dq[u]
        out[u, 1] = (both[:, :HD] * SCALE).astype(BF)
        out[u, 2] = both[:, HD:].astype(BF)


def on_device(queries, key_states, value_states, out_grad):
    swap = lax.axis_index("h").astype(jnp.int32).reshape(1)
    shape = jax.ShapeDtypeStruct
    both = (FRAMES, BLK, 2 * HD)
    wrapped = pltpu.VMEM(((FRAMES + 2) * BLK, 2 * HD), BF)
    summed = pltpu.VMEM(((FRAMES + 2) * BLK, 2 * HD), F32)
    diag = pltpu.VMEM((FRAMES, 2 * BLK, 2 * HD), BF)
    mats = 2 * BLK * BLK * HD * FRAMES * 3

    packed = call(
        pack_kernel,
        [pltpu.VMEM((FRAMES, 2, BLK, 2 * HD), BF)],
        (swap, queries, out_grad, key_states, value_states),
        scratch=(pltpu.VMEM((4, BLK, FRAMES * HD), BF), pltpu.SemaphoreType.DMA((4, 4))),
        smem=1,
        space=HBM,
        limit=0,
    )[0]
    tile = lax.all_to_all(packed, ("x", "l"), 0, 0)
    keys_values = tile[:, 1]
    far_keys = move(keys_values, OVER_Z)
    core_keys = move(keys_values, CORE)
    sums, queries_grads, own_diag, own_wrap, own_kt = call(
        own_sums_kernel,
        [
            shape((3, FRAMES, BLK), F32),
            shape(both, BF),
            shape((FRAMES, 2 * BLK, 2 * HD), BF),
            shape(((FRAMES + 2) * BLK, 2 * HD), BF),
            shape((HD, (FRAMES + 2) * BLK), BF),
        ],
        (tile,),
        flops=2 * mats,
    )
    far_queries = move(queries_grads, OVER_Z)
    core_queries = move(queries_grads, CORE)
    final = call(
        side_sums_kernel,
        [shape((2, FRAMES, BLK), F32)],
        (own_diag, far_keys, core_keys, sums),
        scratch=(wrapped, wrapped),
        flops=4 * mats,
    )[0]
    far_final = move(final, OVER_Z)
    core_final = move(final, CORE)
    part, dq = call(
        near_queries_kernel,
        [shape(both, F32), shape((FRAMES, BLK, HD), BF)],
        (own_diag, own_wrap, own_kt, core_keys, far_keys, final, core_queries, core_final),
        scratch=(
            diag,
            wrapped,
            wrapped,
            pltpu.VMEM((2, HD, (FRAMES + 2) * BLK), BF),
            summed,
        ),
        flops=15 * mats,
    )
    grads = call(
        far_queries_kernel,
        [shape((FRAMES, 3, BLK, HD), BF)],
        (own_wrap, far_queries, far_final, part, dq),
        scratch=(diag, summed),
        flops=4 * mats,
    )[0]
    back = lax.all_to_all(grads, ("x", "l"), 0, 0)
    flat = shape((1, BLK, FRAMES * HD), BF)
    return tuple(
        call(
            unpack_kernel,
            [flat] * 3,
            (swap, back),
            scratch=(pltpu.VMEM((3, BLK, FRAMES * HD), BF), pltpu.SemaphoreType.DMA((3, 4))),
            smem=1,
            out_space=HBM,
        )
    )


def solution(mesh):
    fine = jax.sharding.Mesh(mesh.devices.reshape(SIZES), AXES)
    placed = P(("x", "l"), ("h", "z", "c"), None)
    return jax.shard_map(
        on_device,
        mesh=fine,
        in_specs=(placed,) * 4,
        out_specs=(placed,) * 3,
        check_vma=False,
    )
```
